1024 devices in a mesh: row: 256 (over y, z, core), col: 4 (over x).
Axes of the slice: x: 4, y: 4, z: 32, core: 2. Of those that a mesh axis runs over, the one named last changes fastest.
Arguments:
- a_tiles: bfloat16 [4096, 8, 128, 128], P('row', 'col'), may hold values from -0.5 to 0.5
- a_cols: int32 [4096, 8], P('row', 'col'), may hold values from 0 to 4095, as said below
- p_tiles: bfloat16 [4096, 3, 128, 128], P('row'), may hold values from -0.5 to 0.5
- p_cols: int32 [4096, 3], replicated, may hold values from 0 to 1023, as said below
- c_cols: int32 [1024, 8], replicated, may hold values from 0 to 1023, as said below
Outputs:
- coarse: float32 [1024, 8, 128, 128], P('row', None, 'col')
The draws below stay inside these ranges and needn't reach their ends.
Inputs may be any that keep to these rules, and one draw needn't show every extreme that they name: `a_cols`: a row's entries are distinct and lie within 8 of the row's own index. `p_cols`: a row's entries are distinct and lie within 2 of the row's index times 4 // 16. `c_cols`: a row's entries are distinct and lie within 8 of the row's own index.
All inputs are finite; a program needn't handle non-finite values.
Results may differ from the reference program's by a relative error of at most 0.0029.
Values may be sent and summed in bfloat16 or wider, within the bound.
A program may use at most 32 MiB of HBM per device.

```python
import jax
import jax.numpy as jnp
from jax import lax

BS = 128
RB = 16
KP = 3
KC = 8
KA = 8
CB = 4
NF = 4096
NC = 1024


def choose_near(key, centre, spread, limit, count, weight):
    offsets = jnp.arange(-spread, spread + 1, dtype=jnp.int32)
    candidate = centre[:, None] + offsets[None, :]
    valid = (candidate >= 0) & (candidate < limit)
    noise = jax.random.randint(key, candidate.shape, 0, 64, dtype=jnp.int32)
    score = noise + weight * jnp.abs(offsets)[None, :] + jnp.where(valid, 0, 100000)
    score = score * (2 * spread + 2) + jnp.arange(2 * spread + 1, dtype=jnp.int32)[None, :]
    order = jnp.argsort(score, axis=-1, stable=True)[:, :count]
    return jnp.take_along_axis(candidate, order, axis=-1).astype(jnp.int32)


def draw_a_cols(key, part):
    key = jax.random.fold_in(key, 1)
    centre = jnp.arange(NF, dtype=jnp.int32)
    return choose_near(key, centre, KA, NF, KA, 0)


def draw_p_cols(key, part):
    key = jax.random.fold_in(key, 2)
    centre = jnp.arange(NF, dtype=jnp.int32) * CB // RB
    return choose_near(key, centre, 2, NC, KP, 0)


def draw_c_cols(key, part):
    key = jax.random.fold_in(key, 3)
    centre = jnp.arange(NC, dtype=jnp.int32)
    return choose_near(key, centre, KC, NC, KC, 8)


def steps_of(stream_key, dims, shards, least, largest):
    loudness = 1.0
    for dim, shards_of in shards:
        draws = jax.random.uniform(jax.random.fold_in(jax.random.fold_in(stream_key, 6), dim), (shards_of,), jnp.float32, least / len(shards), largest / len(shards))
        loudness = loudness * jnp.repeat(jnp.exp(draws), dims[dim] // shards_of).reshape((-1,) + (1,) * (len(dims) - 1 - dim))
    return loudness


def bell_draw(own_key, extent, scale, most, split=(), kind=jnp.bfloat16):
    entries = scale * jax.random.normal(own_key, extent, jnp.float32)
    if split:
        entries = entries * steps_of(own_key, extent, split, -0.22, 0.18)
    return jnp.clip(entries, -most, most).astype(kind)


def setup_inputs(seed: int = 0) -> dict:
    streams_of = jax.random.split(jax.random.key(seed), 6)
    a_tiles = bell_draw(streams_of[0], (NF, KA, BS, BS), BS ** -0.5, 0.5, ((0, 256), (1, 4)))
    a_cols = draw_a_cols(jax.random.fold_in(streams_of[5], 71), 0)
    p_tiles = bell_draw(streams_of[2], (NF, KP, BS, BS), BS ** -0.5, 0.5, ((0, 256),))
    p_cols = draw_p_cols(jax.random.fold_in(streams_of[5], 71), 0)
    c_cols = draw_c_cols(jax.random.fold_in(streams_of[5], 71), 0)
    return {"a_tiles": a_tiles, "a_cols": a_cols, "p_tiles": p_tiles, "p_cols": p_cols, "c_cols": c_cols}


def reference(a_tiles, a_cols, p_tiles, p_cols, c_cols):
    fine_count = a_tiles.shape[0]
    width = a_tiles.shape[2]
    coarse_count = c_cols.shape[0]
    pattern_len = c_cols.shape[1]
    dummy = coarse_count * pattern_len
    slot_ids = jnp.arange(pattern_len, dtype=jnp.int32)

    def step(acc, row_id):
        tiles = a_tiles[row_id].astype(jnp.float32)
        interp = p_tiles[row_id].astype(jnp.float32)
        left = jnp.einsum('pkx,aky->paxy', interp, tiles, precision=lax.Precision.HIGHEST).astype(jnp.bfloat16)
        columns = a_cols[row_id]
        remote = p_tiles[columns].astype(jnp.float32)
        term = jnp.einsum('paxk,aqky->paqxy', left.astype(jnp.float32), remote, precision=lax.Precision.HIGHEST)
        coarse_i = p_cols[row_id]
        coarse_j = p_cols[columns]
        pattern = c_cols[coarse_i]
        match = pattern[:, None, None, :] == coarse_j[None, :, :, None]
        found = jnp.any(match, axis=-1)
        slot = jnp.sum(jnp.where(match, slot_ids, 0), axis=-1).astype(jnp.int32)
        flat = jnp.where(found, coarse_i[:, None, None] * pattern_len + slot, dummy).astype(jnp.int32)
        acc = acc.at[flat.reshape(-1)].add(term.reshape(-1, width, width))
        return acc, None

    start = jnp.zeros((dummy + 1, width, width), jnp.float32)
    acc, _ = lax.scan(step, start, jnp.arange(fine_count, dtype=jnp.int32))
    return acc[:dummy].reshape(coarse_count, pattern_len, width, width)
```

```python
import functools

import jax
import jax.numpy as jnp
from jax import lax
from jax.experimental import pallas as pl
from jax.experimental.pallas import tpu as pltpu
from jax.sharding import PartitionSpec as P

MESH = pl.DeviceIdType.MESH
BS = 128
RB = 16
KP = 3
KA = 2
KC = 8
HALO = 8
GROUPS = 4
GR = 4
WI = 5
WC = 9
NI = 8
NK = 12
HT = HALO * KP
LT = RB * KP
ZERO_TILE = 2 * HT + LT
F32 = jnp.float32
BF16 = jnp.bfloat16


def select_slot(wanted, columns, values, otherwise):
    picked = jnp.int32(otherwise)
    for column, value in zip(columns, values):
        picked = jnp.where(column == wanted, value, picked)
    return picked


def kernel(
    rows, cols,
    a_cols_ref, p_cols_ref, c_cols_ref, a_ref, p_ref,
    out_ref,
    ac, pc, cc, p_buf, a_buf, left, lhs, rhs, acc, edge_out, edge_in, own, part_out, part_in,
    local_sem, halo_send, halo_recv, edge_send, edge_recv, part_send, part_recv,
):
    r = lax.axis_index("row")
    x = lax.axis_index("col")
    core = lax.rem(r, 2)
    before = lax.rem(r + rows - 1, rows)
    after = lax.rem(r + 1, rows)
    far = jnp.where(core == 0, before, after)
    near = jnp.where(core == 0, after, before)

    local = [
        pltpu.make_async_copy(src, dst, local_sem.at[i])
        for i, (src, dst) in enumerate((
            (p_ref, p_buf.at[pl.ds(HT, LT)]),
            (a_ref, a_buf),
            (a_cols_ref, ac),
            (p_cols_ref, pc),
            (c_cols_ref, cc),
        ))
    ]
    for copy in local:
        copy.start()

    barrier = pltpu.get_barrier_semaphore()
    for target in (before, after):
        pl.semaphore_signal(barrier, inc=1, device_id={"row": target}, device_id_type=MESH)
    for d in range(1, cols):
        pl.semaphore_signal(
            barrier, inc=1, device_id={"col": lax.rem(x + d, cols)}, device_id_type=MESH
        )
    pl.semaphore_wait(barrier, 2 + cols - 1)

    halo = [
        pltpu.make_async_remote_copy(
            src_ref=p_ref.at[pl.ds(src, HT)],
            dst_ref=p_buf.at[pl.ds(dst, HT)],
            send_sem=halo_send.at[i],
            recv_sem=halo_recv.at[i],
            device_id={"row": target},
            device_id_type=MESH,
        )
        for i, (src, dst, target) in enumerate(((0, HT + LT, before), (LT - HT, 0, after)))
    ]
    for copy in halo:
        copy.start()

    p_buf[ZERO_TILE] = jnp.zeros((BS, BS), BF16)

    def clear_acc(k, _):
        acc[k] = jnp.zeros((NI * BS, BS), F32)
        return 0

    lax.fori_loop(0, NK + 1, clear_acc, 0)
    local[0].wait()
    local[1].wait()

    def make_left(g, _):
        tiles = jnp.concatenate([a_buf[g * KA + a] for a in range(KA)], axis=1)
        for p in range(KP):
            left[g * (KP + 1) + p] = lax.dot_general(
                p_buf[HT + g * KP + p], tiles, (((0,), (0,)), ((), ())),
                preferred_element_type=F32,
            ).astype(BF16)
        left[g * (KP + 1) + KP] = jnp.zeros((BS, KA * BS), BF16)
        return 0

    lax.fori_loop(0, RB, make_left, 0)
    for copy in local[2:]:
        copy.wait()

    def make_lhs(gi, _):
        for gg in range(GR):
            g = gi * GR + gg
            columns = [pc[p, r * RB + g] for p in range(KP)]
            for s in range(WI):
                slot = select_slot(r * GROUPS - 2 + gi + s, columns, range(KP), KP)
                lhs[gi, s * BS:(s + 1) * BS, gg * KA * BS:(gg + 1) * KA * BS] = (
                    left[g * (KP + 1) + slot]
                )
        return 0

    lax.fori_loop(0, GROUPS, make_lhs, 0)
    for copy in halo:
        copy.wait()

    def group(t, _):
        gi = jnp.where(core == 0, t, GROUPS - 1 - t)
        for gg in range(GR):
            g = gi * GR + gg
            for a in range(KA):
                j = ac[a, g]
                columns = [pc[q, j] for q in range(KP)]
                first = jnp.clip(j - (r * RB - HALO), 0, RB + 2 * HALO - 1) * KP
                values = [first + q for q in range(KP)]
                for w in range(WC):
                    tile = select_slot(r * GROUPS - 4 + gi + w, columns, values, ZERO_TILE)
                    at = (gg * KA + a) * BS
                    rhs[at:at + BS, w * BS:(w + 1) * BS] = p_buf[tile]
        i_rows = pl.ds(pl.multiple_of(gi * BS, BS), WI * BS)
        for w in range(0, WC, 2):
            wide = min(2, WC - w)
            piece = jnp.dot(
                lhs[gi], rhs[:, w * BS:(w + wide) * BS], preferred_element_type=F32
            )
            for u in range(wide):
                acc[gi + w + u, i_rows, :] += piece[:, u * BS:(u + 1) * BS]
        return 0

    def tile_of(row, s):
        i = r * GROUPS - 2 + row
        i = jnp.clip(i, 0, rows * GROUPS - 1)
        k = cc[s, i] - (r * GROUPS - 4)
        k = jnp.where(jnp.logical_and(k >= 0, k < NK), k, NK)
        return acc[k, pl.ds(pl.multiple_of(row * BS, BS), BS), :]

    def send_edge(side, first_row, target):
        def one(n, _):
            i, s = n // KC, n % KC
            edge_out[side, n] = tile_of(first_row + i, s).astype(BF16)
            return 0

        lax.fori_loop(0, 2 * KC, one, 0)
        copy = pltpu.make_async_remote_copy(
            src_ref=edge_out.at[side],
            dst_ref=edge_in.at[side],
            send_sem=edge_send.at[side],
            recv_sem=edge_recv.at[side],
            device_id={"row": target},
            device_id_type=MESH,
        )
        copy.start()
        return copy

    lax.fori_loop(0, 2, group, 0)
    far_edge = send_edge(0, jnp.where(core == 0, 0, 6), far)
    lax.fori_loop(2, 4, group, 0)
    near_edge = send_edge(1, jnp.where(core == 0, 6, 0), near)

    def send_parts(side, first_row):
        def one(n, _):
            i, s = n // KC, n % KC
            total = tile_of(first_row + i, s) + edge_in[side, n].astype(F32)
            own[side, n] = total
            size = BS // cols
            for part in range(cols):
                part_out[side, part, n] = total[part * size:(part + 1) * size].astype(BF16)
            return 0

        lax.fori_loop(0, 2 * KC, one, 0)
        copies = []
        for d in range(1, cols):
            target = lax.rem(x + d, cols)
            copies.append(pltpu.make_async_remote_copy(
                src_ref=part_out.at[side, target],
                dst_ref=part_in.at[side, d - 1],
                send_sem=part_send.at[side, d - 1],
                recv_sem=part_recv.at[side, d - 1],
                device_id={"col": target},
                device_id_type=MESH,
            ))
            copies[-1].start()
        return copies

    near_row = jnp.where(core == 0, 4, 2)
    far_row = jnp.where(core == 0, 2, 4)
    near_edge.wait()
    near_parts = send_parts(1, near_row)
    far_edge.wait()
    far_parts = send_parts(0, far_row)

    def finish(side, first_row, copies):
        for copy in copies:
            copy.wait()
        size = BS // cols
        mine = pl.ds(pl.multiple_of(x * size, size), size)

        def one(n, _):
            i, s = n // KC, n % KC
            total = own[side, n, mine, :]
            for d in range(cols - 1):
                total = total + part_in[side, d, n].astype(F32)
            out_ref[(first_row - 2 + i) * KC + s] = total
            return 0

        lax.fori_loop(0, 2 * KC, one, 0)

    finish(1, near_row, near_parts)
    finish(0, far_row, far_parts)


def per_device(rows, cols, a_tiles, a_cols, p_tiles, p_cols, c_cols):
    size = BS // cols
    dma = pltpu.SemaphoreType.DMA
    hbm = pl.BlockSpec(memory_space=pl.ANY)
    out = pl.pallas_call(
        functools.partial(kernel, rows, cols),
        out_shape=jax.ShapeDtypeStruct((GROUPS * KC, size, BS), F32),
        in_specs=[hbm] * 5,
        out_specs=pl.BlockSpec(memory_space=pltpu.VMEM),
        scratch_shapes=[
            pltpu.SMEM((KA, RB), jnp.int32),
            pltpu.SMEM(p_cols.shape[::-1], jnp.int32),
            pltpu.SMEM(c_cols.shape[::-1], jnp.int32),
            pltpu.VMEM((ZERO_TILE + 1, BS, BS), BF16),
            pltpu.VMEM((RB * KA, BS, BS), BF16),
            pltpu.VMEM((RB * (KP + 1), BS, KA * BS), BF16),
            pltpu.VMEM((GROUPS, WI * BS, GR * KA * BS), BF16),
            pltpu.VMEM((GR * KA * BS, WC * BS), BF16),
            pltpu.VMEM((NK + 1, NI * BS, BS), F32),
            pltpu.VMEM((2, 2 * KC, BS, BS), BF16),
            pltpu.VMEM((2, 2 * KC, BS, BS), BF16),
            pltpu.VMEM((2, 2 * KC, BS, BS), F32),
            pltpu.VMEM((2, cols, 2 * KC, size, BS), BF16),
            pltpu.VMEM((2, cols - 1, 2 * KC, size, BS), BF16),
            dma((5,)),
            dma((2,)),
            dma((2,)),
            dma((2,)),
            dma((2,)),
            dma((2, cols - 1)),
            dma((2, cols - 1)),
        ],
        compiler_params=pltpu.CompilerParams(
            collective_id=0, has_side_effects=True, vmem_limit_bytes=58 * 1024 * 1024
        ),
    )(
        a_cols.T, p_cols.T, c_cols.T,
        a_tiles.reshape(RB * KA, BS, BS), p_tiles.reshape(LT, BS, BS),
    )
    return out.reshape(GROUPS, KC, size, BS)


def solution(mesh):
    rows, cols = mesh.shape["row"], mesh.shape["col"]
    in_specs = (P("row", "col", None, None), P("row", "col"), P("row", None, None, None), P(), P())
    return jax.shard_map(
        functools.partial(per_device, rows, cols),
        mesh=mesh, in_specs=in_specs, out_specs=P("row", None, "col", None), check_vma=False,
    )
```

```python
import functools

import jax
import jax.numpy as jnp
from jax import lax
from jax.experimental import pallas as pl
from jax.experimental.pallas import tpu as pltpu
from jax.sharding import PartitionSpec as P

MESH = pl.DeviceIdType.MESH
BS = 128
RB = 16
KP = 3
KA = 2
KC = 8
HALO = 8
GROUPS = 4
GR = 4
WI = 5
WC = 9
NI = 8
NK = 12
HT = HALO * KP
LT = RB * KP
ZERO_TILE = HT + LT
PAIR = 2 * KC
FAR, NEAR = 0, 1
F32 = jnp.float32
BF16 = jnp.bfloat16


def select_slot(wanted, columns, values, otherwise):
    picked = jnp.int32(otherwise)
    for column, value in zip(columns, values):
        picked = jnp.where(column == wanted, value, picked)
    return picked


def tiles_at(first, count):
    return pl.ds(pl.multiple_of(first * BS, BS), count * BS)


def kernel(
    rows, cols,
    a_cols_ref, p_cols_ref, c_cols_ref, a_ref, p_ref,
    out_ref,
    ac, pc, cc, far_buf, near_buf, a_buf, left, lhs, rhs, acc,
    edge_out, edge_in, own, part_out, merged, part_in, relay_in,
    local_sem, near_send, near_recv, far_send, far_recv, hop_send, hop_recv,
    edge_send, edge_recv, part_send, part_recv,
):
    r = lax.axis_index("row")
    x = lax.axis_index("col")
    first_core = lax.rem(r, 2) == 0

    def by_core(zero, one):
        return jnp.where(first_core, zero, one)

    before = lax.rem(r + rows - 1, rows)
    after = lax.rem(r + 1, rows)
    far = by_core(before, after)
    near = by_core(after, before)
    up = lax.rem(x + 1, cols)
    across = lax.rem(x + 2, cols)
    down = lax.rem(x + 3, cols)

    def send(src, dst, sems, recv_sems, at, **device):
        copy = pltpu.make_async_remote_copy(
            src_ref=src, dst_ref=dst, send_sem=sems.at[at], recv_sem=recv_sems.at[at],
            device_id=device, device_id_type=MESH,
        )
        copy.start()
        return copy

    far_rows = by_core(HT, 0)
    near_rows = by_core(0, HT)
    local = [
        pltpu.make_async_copy(src, dst, local_sem.at[i])
        for i, (src, dst) in enumerate((
            (p_ref, near_buf.at[pl.ds(near_rows, LT)]),
            (a_ref, a_buf),
            (a_cols_ref, ac),
            (p_cols_ref, pc),
            (c_cols_ref, cc),
            (p_ref, far_buf.at[pl.ds(far_rows, LT)]),
        ))
    ]
    for copy in local:
        copy.start()

    barrier = pltpu.get_barrier_semaphore()
    for target in (before, after):
        pl.semaphore_signal(barrier, inc=1, device_id={"row": target}, device_id_type=MESH)
    for target in (up, down):
        pl.semaphore_signal(barrier, inc=1, device_id={"col": target}, device_id_type=MESH)
    pl.semaphore_wait(barrier, 4)

    far_src = by_core(0, LT - HT)
    far_there = by_core(LT, 0)
    far_here = by_core(0, LT)
    far_halo = []
    for k, (row, count) in enumerate(((x, 1), (across, 1), (4, 2), (6, 2))):
        far_halo.append(send(
            p_ref.at[pl.ds(far_src + row * KP, count * KP)],
            far_buf.at[pl.ds(far_there + row * KP, count * KP)],
            far_send, far_recv, k, row=far,
        ))
    near_halo = send(
        p_ref.at[pl.ds(by_core(LT - HT, 0), HT)],
        near_buf.at[pl.ds(by_core(0, LT), HT)],
        near_send, near_recv, 0, row=near,
    )

    far_buf[ZERO_TILE] = jnp.zeros((BS, BS), BF16)
    near_buf[ZERO_TILE] = jnp.zeros((BS, BS), BF16)

    def clear_acc(k, _):
        acc[k] = jnp.zeros((NI * BS, BS), F32)
        return 0

    lax.fori_loop(0, NK + 1, clear_acc, 0)
    local[0].wait()
    local[1].wait()

    def make_left(g, _):
        tiles = jnp.concatenate([a_buf[g * KA + a] for a in range(KA)], axis=1)
        interp = jnp.concatenate(
            [near_buf[near_rows + g * KP + p] for p in range(KP)], axis=1
        )
        product = lax.dot_general(
            interp, tiles, (((0,), (0,)), ((), ())), preferred_element_type=F32
        ).astype(BF16)
        for p in range(KP):
            left[g * (KP + 1) + p] = product[p * BS:(p + 1) * BS]
        left[g * (KP + 1) + KP] = jnp.zeros((BS, KA * BS), BF16)
        return 0

    lax.fori_loop(0, 8, make_left, 0, unroll=2)
    far_halo[0].wait_recv()
    here = far_buf.at[pl.ds(far_here + x * KP, KP)]
    hops = [
        send(here, here, hop_send, hop_recv, n, col=target)
        for n, target in enumerate((up, down))
    ]
    lax.fori_loop(8, RB, make_left, 0, unroll=2)
    for copy in local[2:]:
        copy.wait()

    def make_lhs(gi, _):
        for gg in range(GR):
            g = gi * GR + gg
            columns = [pc[p, r * RB + g] for p in range(KP)]
            for s in range(WI):
                slot = select_slot(r * GROUPS - 2 + gi + s, columns, range(KP), KP)
                lhs[gi, s * BS:(s + 1) * BS, gg * KA * BS:(gg + 1) * KA * BS] = (
                    left[g * (KP + 1) + slot]
                )
        return 0

    lax.fori_loop(0, GROUPS, make_lhs, 0)
    def make_rhs(group):
        gi = by_core(group, GROUPS - 1 - group)
        if group < 2:
            buf, first_row = far_buf, r * RB - by_core(HALO, 0)
        else:
            buf, first_row = near_buf, r * RB - by_core(0, HALO)
        for gg in range(GR):
            for a in range(KA):
                j = ac[a, gi * GR + gg]
                columns = [pc[q, j] for q in range(KP)]
                first = jnp.clip(j - first_row, 0, RB + HALO - 1) * KP
                values = [first + q for q in range(KP)]
                at = (gg * KA + a) * BS
                for w in range(WC):
                    tile = select_slot(r * GROUPS - 4 + gi + w, columns, values, ZERO_TILE)
                    rhs[gi, at:at + BS, w * BS:(w + 1) * BS] = buf[tile]

    def add_block(group, row, count):
        gi = by_core(group, GROUPS - 1 - group)
        i = by_core(row, NI - row - count)
        for w in range(0, WC, 2):
            wide = min(2, WC - w)
            piece = jnp.dot(
                lhs[gi, tiles_at(i - gi, count), :], rhs[gi, :, w * BS:(w + wide) * BS],
                preferred_element_type=F32,
            )
            for u in range(wide):
                acc[gi + w + u, tiles_at(i, count), :] += piece[:, u * BS:(u + 1) * BS]

    def tile_of(row, s):
        i = jnp.clip(r * GROUPS - 2 + row, 0, rows * GROUPS - 1)
        k = cc[s, i] - (r * GROUPS - 4)
        k = jnp.where(jnp.logical_and(k >= 0, k < NK), k, NK)
        return acc[k, tiles_at(row, 1), :]

    def send_edge(side, row, order, target):
        i = by_core(row, NI - 1 - row)

        def one(s, _):
            edge_out[side, lax.rem(i, 2) * KC + s] = tile_of(i, s).astype(BF16)
            return 0

        lax.fori_loop(0, KC, one, 0)
        at = pl.ds(lax.rem(i, 2) * KC, KC)
        return send(
            edge_out.at[side, at], edge_in.at[side, at], edge_send, edge_recv,
            2 * side + order, row=target,
        )

    near_halo.wait()
    make_rhs(3)
    add_block(3, 3, 5)
    near_edges = [send_edge(NEAR, 7, 0, near)]
    for copy in far_halo[1:]:
        copy.wait_recv()
    for copy in far_halo:
        copy.wait_send()
    for copy in hops:
        copy.wait()
    make_rhs(0)
    add_block(0, 0, 2)
    far_edges = [send_edge(FAR, 0, 0, far)]
    make_rhs(1)
    add_block(1, 1, 1)
    far_edges.append(send_edge(FAR, 1, 1, far))
    make_rhs(2)
    add_block(2, 2, 5)
    near_edges.append(send_edge(NEAR, 6, 1, near))
    add_block(1, 4, 2)
    add_block(0, 4, 1)

    size = BS // cols

    def part_of(part):
        return pl.ds(pl.multiple_of(part * size, size), size)

    def send_parts(side, first_row):
        def one(n, _):
            total = tile_of(first_row + n // KC, n % KC) + edge_in[side, n].astype(F32)
            own[side, n] = total
            for part in range(cols):
                part_out[side, part, n] = total[part * size:(part + 1) * size].astype(BF16)
            return 0

        lax.fori_loop(0, PAIR, one, 0)
        relays, direct = [], []
        for way, target in enumerate((up, down)):
            first, last = pl.ds(way * KC, KC), pl.ds((1 - way) * KC, KC)
            relays.append(send(
                part_out.at[side, across, first], relay_in.at[side, way],
                part_send, part_recv, 6 * side + 3 * way, col=target,
            ))
            direct.append(send(
                part_out.at[side, target, last], part_in.at[side, way, last],
                part_send, part_recv, 6 * side + 3 * way + 1, col=target,
            ))
        return relays, direct

    def send_merged(side, relays):
        copies = []
        for way, target in enumerate((up, down)):
            relays[way].wait()

            def one(n, _):
                total = own[side, way * KC + n, part_of(target), :]
                merged[side, way, n] = (total + relay_in[side, way, n].astype(F32)).astype(BF16)
                return 0

            lax.fori_loop(0, KC, one, 0)
            copies.append(send(
                merged.at[side, way], part_in.at[side, way, pl.ds(way * KC, KC)],
                part_send, part_recv, 6 * side + 3 * way + 2, col=target,
            ))
        return copies

    def finish(side, first_row, copies):
        for copy in copies:
            copy.wait()

        def one(n, _):
            total = own[side, n, part_of(x), :]
            for way in range(2):
                total = total + part_in[side, way, n].astype(F32)
            out_ref[(first_row - 2) * KC + n] = total
            return 0

        lax.fori_loop(0, PAIR, one, 0)

    near_row = by_core(4, 2)
    far_row = by_core(2, 4)
    for copy in near_edges:
        copy.wait()
    near_relays, near_direct = send_parts(NEAR, near_row)
    for group, row, count in ((0, 2, 2), (1, 2, 2)):
        add_block(group, row, count)
    near_merged = send_merged(NEAR, near_relays)
    for copy in far_edges:
        copy.wait()
    far_relays, far_direct = send_parts(FAR, far_row)
    far_merged = send_merged(FAR, far_relays)
    finish(NEAR, near_row, near_direct + near_merged)
    finish(FAR, far_row, far_direct + far_merged)


def per_device(rows, cols, a_tiles, a_cols, p_tiles, p_cols, c_cols):
    size = BS // cols
    dma = pltpu.SemaphoreType.DMA
    hbm = pl.BlockSpec(memory_space=pl.ANY)
    out = pl.pallas_call(
        functools.partial(kernel, rows, cols),
        out_shape=pltpu.VMEM((GROUPS * KC, size, BS), F32),
        in_specs=[hbm] * 5,
        out_specs=pl.BlockSpec(memory_space=pltpu.VMEM),
        scratch_shapes=[
            pltpu.SMEM((KA, RB), jnp.int32),
            pltpu.SMEM(p_cols.shape[::-1], jnp.int32),
            pltpu.SMEM(c_cols.shape[::-1], jnp.int32),
            pltpu.VMEM((ZERO_TILE + 1, BS, BS), BF16),
            pltpu.VMEM((ZERO_TILE + 1, BS, BS), BF16),
            pltpu.VMEM((RB * KA, BS, BS), BF16),
            pltpu.VMEM((RB * (KP + 1), BS, KA * BS), BF16),
            pltpu.VMEM((GROUPS, WI * BS, GR * KA * BS), BF16),
            pltpu.VMEM((GROUPS, GR * KA * BS, WC * BS), BF16),
            pltpu.VMEM((NK + 1, NI * BS, BS), F32),
            pltpu.VMEM((2, PAIR, BS, BS), BF16),
            pltpu.VMEM((2, PAIR, BS, BS), BF16),
            pltpu.VMEM((2, PAIR, BS, BS), F32),
            pltpu.VMEM((2, cols, PAIR, size, BS), BF16),
            pltpu.VMEM((2, 2, KC, size, BS), BF16),
            pltpu.VMEM((2, 2, PAIR, size, BS), BF16),
            pltpu.VMEM((2, 2, KC, size, BS), BF16),
            dma((6,)),
            dma((1,)),
            dma((1,)),
            dma((4,)),
            dma((4,)),
            dma((2,)),
            dma((2,)),
            dma((4,)),
            dma((4,)),
            dma((12,)),
            dma((12,)),
        ],
        compiler_params=pltpu.CompilerParams(
            collective_id=0, has_side_effects=True, vmem_limit_bytes=58 * 1024 * 1024
        ),
    )(
        a_cols.T, p_cols.T, c_cols.T,
        a_tiles.reshape(RB * KA, BS, BS), p_tiles.reshape(LT, BS, BS),
    )
    return out.reshape(GROUPS, KC, size, BS)


def solution(mesh):
    rows, cols = mesh.shape["row"], mesh.shape["col"]
    in_specs = (P("row", "col", None, None), P("row", "col"), P("row", None, None, None), P(), P())
    return jax.shard_map(
        functools.partial(per_device, rows, cols),
        mesh=mesh, in_specs=in_specs, out_specs=P("row", None, "col", None), check_vma=False,
    )
```

```python
import functools

import jax
import jax.numpy as jnp
from jax import lax
from jax.experimental import pallas as pl
from jax.experimental.pallas import tpu as pltpu
from jax.sharding import PartitionSpec as P

MESH = pl.DeviceIdType.MESH
BS = 128
RB = 16
KP = 3
KA = 2
KC = 8
HALO = 8
GROUPS = 4
GR = 4
WI = 5
WC = 9
NI = 8
NK = 12
HT = HALO * KP
LT = RB * KP
ZERO_TILE = HT + LT
PAIR = 2 * KC
FAR, NEAR = 0, 1
F32 = jnp.float32
BF16 = jnp.bfloat16


def select_slot(wanted, columns, values, otherwise):
    picked = jnp.int32(otherwise)
    for column, value in zip(columns, values):
        picked = jnp.where(column == wanted, value, picked)
    return picked


def tiles_at(first, count):
    return pl.ds(pl.multiple_of(first * BS, BS), count * BS)


def kernel(
    rows, cols,
    a_cols_ref, p_cols_ref, c_cols_ref, a_ref, p_ref,
    out_ref,
    ac, pc, cc, far_buf, near_buf, a_buf, left, lhs, rhs, acc,
    edge_out, edge_in, own, part_out, merged, part_in, relay_in,
    local_sem, near_send, near_recv, far_send, far_recv, hop_send, hop_recv,
    edge_send, edge_recv, part_send, part_recv,
):
    r = lax.axis_index("row")
    x = lax.axis_index("col")
    first_core = lax.rem(r, 2) == 0

    def by_core(zero, one):
        return jnp.where(first_core, zero, one)

    before = lax.rem(r + rows - 1, rows)
    after = lax.rem(r + 1, rows)
    far = by_core(before, after)
    near = by_core(after, before)
    up = lax.rem(x + 1, cols)
    across = lax.rem(x + 2, cols)
    down = lax.rem(x + 3, cols)

    def send(src, dst, sems, recv_sems, at, **device):
        copy = pltpu.make_async_remote_copy(
            src_ref=src, dst_ref=dst, send_sem=sems.at[at], recv_sem=recv_sems.at[at],
            device_id=device, device_id_type=MESH,
        )
        copy.start()
        return copy

    far_rows = by_core(HT, 0)
    near_rows = by_core(0, HT)
    local = [
        pltpu.make_async_copy(src, dst, local_sem.at[i])
        for i, (src, dst) in enumerate((
            (p_ref, near_buf.at[pl.ds(near_rows, LT)]),
            (a_ref, a_buf),
            (a_cols_ref, ac),
            (p_cols_ref, pc),
            (c_cols_ref, cc),
            (p_ref, far_buf.at[pl.ds(far_rows, LT)]),
        ))
    ]
    for copy in local:
        copy.start()

    barrier = pltpu.get_barrier_semaphore()
    for target in (before, after):
        pl.semaphore_signal(barrier, inc=1, device_id={"row": target}, device_id_type=MESH)
    for target in (up, down):
        pl.semaphore_signal(barrier, inc=1, device_id={"col": target}, device_id_type=MESH)
    pl.semaphore_wait(barrier, 4)

    far_src = by_core(0, LT - HT)
    far_there = by_core(LT, 0)
    far_here = by_core(0, LT)
    far_halo = []
    for k, (tile, count) in enumerate((
        (4 * x, 2), (4 * x + 2, 2), (4 * across, 4), (16, 4), (20, 4)
    )):
        far_halo.append(send(
            p_ref.at[pl.ds(far_src + tile, count)], far_buf.at[pl.ds(far_there + tile, count)],
            far_send, far_recv, k, row=far,
        ))
    near_halo = send(
        p_ref.at[pl.ds(by_core(LT - HT, 0), HT)],
        near_buf.at[pl.ds(by_core(0, LT), HT)],
        near_send, near_recv, 0, row=near,
    )

    far_buf[ZERO_TILE] = jnp.zeros((BS, BS), BF16)
    near_buf[ZERO_TILE] = jnp.zeros((BS, BS), BF16)

    def clear_acc(k, _):
        acc[k] = jnp.zeros((NI * BS, BS), F32)
        return 0

    lax.fori_loop(0, NK + 1, clear_acc, 0)
    local[0].wait()
    local[1].wait()

    def make_left(g, _):
        tiles = jnp.concatenate([a_buf[g * KA + a] for a in range(KA)], axis=1)
        interp = jnp.concatenate(
            [near_buf[near_rows + g * KP + p] for p in range(KP)], axis=1
        )
        product = lax.dot_general(
            interp, tiles, (((0,), (0,)), ((), ())), preferred_element_type=F32
        ).astype(BF16)
        for p in range(KP):
            left[g * (KP + 1) + p] = product[p * BS:(p + 1) * BS]
        left[g * (KP + 1) + KP] = jnp.zeros((BS, KA * BS), BF16)
        return 0

    hops = []

    def forward(k):
        far_halo[k].wait_recv()
        here = far_buf.at[pl.ds(far_here + 4 * x + 2 * k, 2)]
        for n, target in enumerate((up, down)):
            hops.append(send(here, here, hop_send, hop_recv, 2 * k + n, col=target))

    lax.fori_loop(0, RB, make_left, 0, unroll=2)
    forward(0)
    for copy in local[2:]:
        copy.wait()

    def make_lhs(gi, _):
        for gg in range(GR):
            g = gi * GR + gg
            columns = [pc[p, r * RB + g] for p in range(KP)]
            for s in range(WI):
                slot = select_slot(r * GROUPS - 2 + gi + s, columns, range(KP), KP)
                lhs[gi, s * BS:(s + 1) * BS, gg * KA * BS:(gg + 1) * KA * BS] = (
                    left[g * (KP + 1) + slot]
                )
        return 0

    lax.fori_loop(0, GROUPS, make_lhs, 0)
    forward(1)
    def make_rhs(group):
        gi = by_core(group, GROUPS - 1 - group)
        if group < 2:
            buf, first_row = far_buf, r * RB - by_core(HALO, 0)
        else:
            buf, first_row = near_buf, r * RB - by_core(0, HALO)
        for gg in range(GR):
            for a in range(KA):
                j = ac[a, gi * GR + gg]
                columns = [pc[q, j] for q in range(KP)]
                first = jnp.clip(j - first_row, 0, RB + HALO - 1) * KP
                values = [first + q for q in range(KP)]
                at = (gg * KA + a) * BS
                for w in range(WC):
                    tile = select_slot(r * GROUPS - 4 + gi + w, columns, values, ZERO_TILE)
                    rhs[gi, at:at + BS, w * BS:(w + 1) * BS] = buf[tile]

    def add_block(group, row, count):
        gi = by_core(group, GROUPS - 1 - group)
        i = by_core(row, NI - row - count)
        for w in range(0, WC, 2):
            wide = min(2, WC - w)
            piece = jnp.dot(
                lhs[gi, tiles_at(i - gi, count), :], rhs[gi, :, w * BS:(w + wide) * BS],
                preferred_element_type=F32,
            )
            for u in range(wide):
                acc[gi + w + u, tiles_at(i, count), :] += piece[:, u * BS:(u + 1) * BS]

    def tile_of(row, s):
        i = jnp.clip(r * GROUPS - 2 + row, 0, rows * GROUPS - 1)
        k = cc[s, i] - (r * GROUPS - 4)
        k = jnp.where(jnp.logical_and(k >= 0, k < NK), k, NK)
        return acc[k, tiles_at(row, 1), :]

    def send_edge(side, row, first, count, order, target):
        i = by_core(row, NI - 1 - row)
        slot = lax.rem(i, 2) * KC + first

        def one(s, _):
            edge_out[side, slot + s] = tile_of(i, first + s).astype(BF16)
            return 0

        lax.fori_loop(0, count, one, 0, unroll=4)
        at = pl.ds(slot, count)
        return send(
            edge_out.at[side, at], edge_in.at[side, at], edge_send, edge_recv,
            order, row=target,
        )

    near_halo.wait()
    make_rhs(3)
    add_block(3, 3, 5)
    near_edges = [send_edge(NEAR, 7, 0, KC, 0, near)]
    make_rhs(2)
    add_block(2, 2, 5)
    near_edges.append(send_edge(NEAR, 6, 0, KC, 1, near))
    for copy in far_halo[2:]:
        copy.wait_recv()
    for copy in hops:
        copy.wait()
    size = BS // cols
    half = KC // 2

    def part_of(part):
        return pl.ds(pl.multiple_of(part * size, size), size)

    def make_parts(order, side, row, first, count):
        i = by_core(row, NI - 1 - row)
        slot = lax.rem(i, 2) * KC

        def one(s, _):
            total = tile_of(i, s) + edge_in[side, slot + s].astype(F32)
            own[order, s] = total
            for part in range(cols):
                part_out[order, part, s] = total[part * size:(part + 1) * size].astype(BF16)
            return 0

        lax.fori_loop(first, first + count, one, 0, unroll=4)

    def send_part(src, dst, order, at, target):
        return send(src, dst, part_send, part_recv, order * 6 + at, col=target)

    def send_halves(order):
        relays, direct = [], []
        for way, target in enumerate((up, down)):
            first, last = pl.ds(way * half, half), pl.ds((1 - way) * half, half)
            relays.append(send_part(
                part_out.at[order, across, first], relay_in.at[order, way], order, way, target
            ))
            direct.append(send_part(
                part_out.at[order, target, last], part_in.at[order, way, last],
                order, 2 + way, target,
            ))
        return relays, direct

    def send_merged(order, relays):
        copies = []
        for way, target in enumerate((up, down)):
            relays[way].wait()

            def one(n, _):
                total = own[order, way * half + n, part_of(target), :]
                merged[order, way, n] = (
                    total + relay_in[order, way, n].astype(F32)
                ).astype(BF16)
                return 0

            lax.fori_loop(0, half, one, 0, unroll=4)
            copies.append(send_part(
                merged.at[order, way], part_in.at[order, way, pl.ds(way * half, half)],
                order, 4 + way, target,
            ))
        return copies

    def send_whole(order, first, count, base):
        some = pl.ds(first, count)
        return [
            send_part(
                part_out.at[order, target, some], part_in.at[order, at, some],
                order, base + at, target,
            )
            for at, target in ((2, across), (0, up), (1, down))
        ]

    def finish(order, row, first, count, arrivals, copies):
        for copy in copies:
            copy.wait()
        i = by_core(row, NI - 1 - row)

        def one(s, _):
            total = own[order, s, part_of(x), :]
            for at in range(arrivals):
                total = total + part_in[order, at, s].astype(F32)
            out_ref[(i - 2) * KC + s] = total
            return 0

        lax.fori_loop(first, first + count, one, 0, unroll=4)

    make_rhs(0)
    add_block(0, 0, 1)
    far_edges = [send_edge(FAR, 0, 0, KC, 2, far)]
    make_rhs(1)
    add_block(1, 4, 2)
    for copy in near_edges:
        copy.wait()
    make_parts(0, NEAR, 5, 0, KC)
    relays0, direct0 = send_halves(0)
    add_block(0, 1, 1)
    add_block(1, 1, 1)
    for n in range(2):
        far_edges.append(send_edge(FAR, 1, n * half, half, 3 + n, far))
    add_block(0, 4, 1)
    make_parts(1, NEAR, 4, 0, KC)
    relays1, direct1 = send_halves(1)
    add_block(0, 2, 2)
    add_block(1, 2, 2)
    merged0 = send_merged(0, relays0)
    far_edges[0].wait()
    make_parts(2, FAR, 3, 0, KC)
    relays2, direct2 = send_halves(2)
    merged1 = send_merged(1, relays1)
    whole3 = []
    for n in range(2):
        far_edges[1 + n].wait()
        make_parts(3, FAR, 2, n * half, half)
        whole3.append(send_whole(3, n * half, half, 3 * n))
    merged2 = send_merged(2, relays2)
    finish(0, 5, 0, KC, 2, direct0 + merged0)
    finish(1, 4, 0, KC, 2, direct1 + merged1)
    finish(2, 3, 0, KC, 2, direct2 + merged2)
    for n in range(2):
        finish(3, 2, n * half, half, 3, whole3[n])
    for copy in far_halo:
        copy.wait_send()


def per_device(rows, cols, a_tiles, a_cols, p_tiles, p_cols, c_cols):
    size = BS // cols
    dma = pltpu.SemaphoreType.DMA
    hbm = pl.BlockSpec(memory_space=pl.ANY)
    out = pl.pallas_call(
        functools.partial(kernel, rows, cols),
        out_shape=pltpu.VMEM((GROUPS * KC, size, BS), F32),
        in_specs=[hbm] * 5,
        out_specs=pl.BlockSpec(memory_space=pltpu.VMEM),
        scratch_shapes=[
            pltpu.SMEM((KA, RB), jnp.int32),
            pltpu.SMEM(p_cols.shape[::-1], jnp.int32),
            pltpu.SMEM(c_cols.shape[::-1], jnp.int32),
            pltpu.VMEM((ZERO_TILE + 1, BS, BS), BF16),
            pltpu.VMEM((ZERO_TILE + 1, BS, BS), BF16),
            pltpu.VMEM((RB * KA, BS, BS), BF16),
            pltpu.VMEM((RB * (KP + 1), BS, KA * BS), BF16),
            pltpu.VMEM((GROUPS, WI * BS, GR * KA * BS), BF16),
            pltpu.VMEM((GROUPS, GR * KA * BS, WC * BS), BF16),
            pltpu.VMEM((NK + 1, NI * BS, BS), F32),
            pltpu.VMEM((2, PAIR, BS, BS), BF16),
            pltpu.VMEM((2, PAIR, BS, BS), BF16),
            pltpu.VMEM((4, KC, BS, BS), F32),
            pltpu.VMEM((4, cols, KC, size, BS), BF16),
            pltpu.VMEM((4, 2, KC // 2, size, BS), BF16),
            pltpu.VMEM((4, cols - 1, KC, size, BS), BF16),
            pltpu.VMEM((4, 2, KC // 2, size, BS), BF16),
            dma((6,)),
            dma((1,)),
            dma((1,)),
            dma((5,)),
            dma((5,)),
            dma((4,)),
            dma((4,)),
            dma((5,)),
            dma((5,)),
            dma((24,)),
            dma((24,)),
        ],
        compiler_params=pltpu.CompilerParams(
            collective_id=0, has_side_effects=True, vmem_limit_bytes=58 * 1024 * 1024
        ),
    )(
        a_cols.T, p_cols.T, c_cols.T,
        a_tiles.reshape(RB * KA, BS, BS), p_tiles.reshape(LT, BS, BS),
    )
    return out.reshape(GROUPS, KC, size, BS)


def solution(mesh):
    rows, cols = mesh.shape["row"], mesh.shape["col"]
    in_specs = (P("row", "col", None, None), P("row", "col"), P("row", None, None, None), P(), P())
    return jax.shard_map(
        functools.partial(per_device, rows, cols),
        mesh=mesh, in_specs=in_specs, out_specs=P("row", None, "col", None), check_vma=False,
    )
```

```python
import functools

import jax
import jax.numpy as jnp
from jax import lax
from jax.experimental import pallas as pl
from jax.experimental.pallas import tpu as pltpu
from jax.sharding import PartitionSpec as P

MESH = pl.DeviceIdType.MESH
BS = 128
RB = 16
KP = 3
KA = 2
KC = 8
HALO = 8
GROUPS = 4
GR = 4
WI = 5
WC = 9
NI = 8
NK = 12
HT = HALO * KP
LT = RB * KP
ZERO_TILE = HT + LT
PAIR = 2 * KC
FAR, NEAR = 0, 1
F32 = jnp.float32
BF16 = jnp.bfloat16


def select_slot(wanted, columns, values, otherwise):
    picked = jnp.int32(otherwise)
    for column, value in zip(columns, values):
        picked = jnp.where(column == wanted, value, picked)
    return picked


class Guarded:
    def __init__(self, copy, made):
        self.copy, self.made = copy, made

    def start(self):
        pl.when(self.made)(self.copy.start)

    def wait(self):
        pl.when(self.made)(self.copy.wait)

    def wait_recv(self):
        pl.when(self.made)(self.copy.wait_recv)

    def wait_send(self):
        pl.when(self.made)(self.copy.wait_send)


def tiles_at(first, count):
    return pl.ds(pl.multiple_of(first * BS, BS), count * BS)


def kernel(
    rows, cols,
    a_cols_ref, p_cols_ref, c_cols_ref, a_ref, p_ref,
    out_ref,
    ac, pc, cc, far_buf, near_buf, a_buf, left, lhs, rhs, acc,
    edge_out, edge_in, own, part_out, merged, part_in, relay_in,
    local_sem, near_send, near_recv, far_send, far_recv, hop_send, hop_recv,
    edge_send, edge_recv, part_send, part_recv,
):
    r = lax.axis_index("row")
    x = lax.axis_index("col")
    first_core = lax.rem(r, 2) == 0

    def by_core(zero, one):
        return jnp.where(first_core, zero, one)

    before = lax.rem(r + rows - 1, rows)
    after = lax.rem(r + 1, rows)
    far = by_core(before, after)
    near = by_core(after, before)
    up = lax.rem(x + 1, cols)
    across = lax.rem(x + 2, cols)
    down = lax.rem(x + 3, cols)

    has_far = by_core(r, rows - 1 - r) > 0

    def send(src, dst, sems, recv_sems, at, made=None, **device):
        copy = pltpu.make_async_remote_copy(
            src_ref=src, dst_ref=dst, send_sem=sems.at[at], recv_sem=recv_sems.at[at],
            device_id=device, device_id_type=MESH,
        )
        if made is not None:
            copy = Guarded(copy, made)
        copy.start()
        return copy

    far_rows = by_core(HT, 0)
    near_rows = by_core(0, HT)
    local = [
        pltpu.make_async_copy(src, dst, local_sem.at[i])
        for i, (src, dst) in enumerate((
            (p_ref, near_buf.at[pl.ds(near_rows, LT)]),
            (a_ref, a_buf),
            (a_cols_ref, ac),
            (p_cols_ref, pc),
            (c_cols_ref, cc),
            (p_ref, far_buf.at[pl.ds(far_rows, LT)]),
        ))
    ]
    for copy in local:
        copy.start()

    barrier = pltpu.get_barrier_semaphore()

    @pl.when(has_far)
    def _():
        pl.semaphore_signal(barrier, inc=1, device_id={"row": far}, device_id_type=MESH)

    pl.semaphore_signal(barrier, inc=1, device_id={"row": near}, device_id_type=MESH)
    for target in (up, down):
        pl.semaphore_signal(barrier, inc=1, device_id={"col": target}, device_id_type=MESH)
    pl.semaphore_wait(barrier, jnp.where(has_far, 4, 3))

    far_src = by_core(0, LT - HT)
    far_there = by_core(LT, 0)
    far_here = by_core(0, LT)
    far_halo = []
    for k, (tile, count) in enumerate((
        (4 * x, 2), (4 * x + 2, 2), (4 * across, 4), (16, 4), (20, 4)
    )):
        far_halo.append(send(
            p_ref.at[pl.ds(far_src + tile, count)], far_buf.at[pl.ds(far_there + tile, count)],
            far_send, far_recv, k, made=has_far, row=far,
        ))
    near_halo = send(
        p_ref.at[pl.ds(by_core(LT - HT, 0), HT)],
        near_buf.at[pl.ds(by_core(0, LT), HT)],
        near_send, near_recv, 0, row=near,
    )

    @pl.when(jnp.logical_not(has_far))
    def _():
        edge_in[FAR] = jnp.zeros((PAIR, BS, BS), BF16)

    far_buf[ZERO_TILE] = jnp.zeros((BS, BS), BF16)
    near_buf[ZERO_TILE] = jnp.zeros((BS, BS), BF16)

    def clear_acc(k, _):
        acc[k] = jnp.zeros((NI * BS, BS), F32)
        return 0

    lax.fori_loop(0, NK + 1, clear_acc, 0)
    local[0].wait()
    local[1].wait()

    def make_left(g, _):
        tiles = jnp.concatenate([a_buf[g * KA + a] for a in range(KA)], axis=1)
        interp = jnp.concatenate(
            [near_buf[near_rows + g * KP + p] for p in range(KP)], axis=1
        )
        product = lax.dot_general(
            interp, tiles, (((0,), (0,)), ((), ())), preferred_element_type=F32
        ).astype(BF16)
        for p in range(KP):
            left[g * (KP + 1) + p] = product[p * BS:(p + 1) * BS]
        left[g * (KP + 1) + KP] = jnp.zeros((BS, KA * BS), BF16)
        return 0

    hops = []

    def forward(k):
        far_halo[k].wait_recv()
        here = far_buf.at[pl.ds(far_here + 4 * x + 2 * k, 2)]
        for n, target in enumerate((up, down)):
            hops.append(
                send(here, here, hop_send, hop_recv, 2 * k + n, made=has_far, col=target)
            )

    lax.fori_loop(0, RB, make_left, 0, unroll=2)
    forward(0)
    for copy in local[2:]:
        copy.wait()

    def make_lhs(gi, _):
        for gg in range(GR):
            g = gi * GR + gg
            columns = [pc[p, r * RB + g] for p in range(KP)]
            for s in range(WI):
                slot = select_slot(r * GROUPS - 2 + gi + s, columns, range(KP), KP)
                lhs[gi, s * BS:(s + 1) * BS, gg * KA * BS:(gg + 1) * KA * BS] = (
                    left[g * (KP + 1) + slot]
                )
        return 0

    lax.fori_loop(0, GROUPS, make_lhs, 0)
    forward(1)
    def make_rhs(group):
        gi = by_core(group, GROUPS - 1 - group)
        if group < 2:
            buf, first_row = far_buf, r * RB - by_core(HALO, 0)
        else:
            buf, first_row = near_buf, r * RB - by_core(0, HALO)
        for gg in range(GR):
            for a in range(KA):
                j = ac[a, gi * GR + gg]
                columns = [pc[q, j] for q in range(KP)]
                first = jnp.clip(j - first_row, 0, RB + HALO - 1) * KP
                values = [first + q for q in range(KP)]
                at = (gg * KA + a) * BS
                for w in range(WC):
                    tile = select_slot(r * GROUPS - 4 + gi + w, columns, values, ZERO_TILE)
                    rhs[gi, at:at + BS, w * BS:(w + 1) * BS] = buf[tile]

    def add_block(group, row, count):
        gi = by_core(group, GROUPS - 1 - group)
        i = by_core(row, NI - row - count)
        for w in range(0, WC, 2):
            wide = min(2, WC - w)
            piece = jnp.dot(
                lhs[gi, tiles_at(i - gi, count), :], rhs[gi, :, w * BS:(w + wide) * BS],
                preferred_element_type=F32,
            )
            for u in range(wide):
                acc[gi + w + u, tiles_at(i, count), :] += piece[:, u * BS:(u + 1) * BS]

    def tile_of(row, s):
        i = jnp.clip(r * GROUPS - 2 + row, 0, rows * GROUPS - 1)
        k = cc[s, i] - (r * GROUPS - 4)
        k = jnp.where(jnp.logical_and(k >= 0, k < NK), k, NK)
        return acc[k, tiles_at(row, 1), :]

    def send_edge(side, row, first, count, order, target):
        i = by_core(row, NI - 1 - row)
        slot = lax.rem(i, 2) * KC + first

        def one(s, _):
            edge_out[side, slot + s] = tile_of(i, first + s).astype(BF16)
            return 0

        lax.fori_loop(0, count, one, 0, unroll=4)
        at = pl.ds(slot, count)
        return send(
            edge_out.at[side, at], edge_in.at[side, at], edge_send, edge_recv,
            order, made=has_far if side == FAR else None, row=target,
        )

    near_halo.wait()
    make_rhs(3)
    add_block(3, 3, 5)
    near_edges = [send_edge(NEAR, 7, 0, KC, 0, near)]
    make_rhs(2)
    add_block(2, 4, 3)
    near_edges.append(send_edge(NEAR, 6, 0, KC, 1, near))
    for copy in far_halo[2:]:
        copy.wait_recv()
    for copy in hops:
        copy.wait()
    size = BS // cols
    half = KC // 2

    def part_of(part):
        return pl.ds(pl.multiple_of(part * size, size), size)

    def make_parts(order, side, row, first, count):
        i = by_core(row, NI - 1 - row)
        slot = lax.rem(i, 2) * KC

        def one(s, _):
            total = tile_of(i, s) + edge_in[side, slot + s].astype(F32)
            own[order, s] = total
            for part in range(cols):
                part_out[order, part, s] = total[part * size:(part + 1) * size].astype(BF16)
            return 0

        lax.fori_loop(first, first + count, one, 0, unroll=4)

    def send_part(src, dst, order, at, target):
        return send(src, dst, part_send, part_recv, order * 6 + at, col=target)

    def send_halves(order):
        relays, direct = [], []
        for way, target in enumerate((up, down)):
            first, last = pl.ds(way * half, half), pl.ds((1 - way) * half, half)
            relays.append(send_part(
                part_out.at[order, across, first], relay_in.at[order, way], order, way, target
            ))
            direct.append(send_part(
                part_out.at[order, target, last], part_in.at[order, way, last],
                order, 2 + way, target,
            ))
        return relays, direct

    def send_merged(order, relays):
        copies = []
        for way, target in enumerate((up, down)):
            relays[way].wait()

            def one(n, _):
                total = own[order, way * half + n, part_of(target), :]
                merged[order, way, n] = (
                    total + relay_in[order, way, n].astype(F32)
                ).astype(BF16)
                return 0

            lax.fori_loop(0, half, one, 0, unroll=4)
            copies.append(send_part(
                merged.at[order, way], part_in.at[order, way, pl.ds(way * half, half)],
                order, 4 + way, target,
            ))
        return copies

    def send_whole(order, first, count, base):
        some = pl.ds(first, count)
        return [
            send_part(
                part_out.at[order, target, some], part_in.at[order, at, some],
                order, base + at, target,
            )
            for at, target in ((2, across), (0, up), (1, down))
        ]

    def finish(order, row, first, count, arrivals, copies):
        for copy in copies:
            copy.wait()
        i = by_core(row, NI - 1 - row)

        def one(s, _):
            total = own[order, s, part_of(x), :]
            for at in range(arrivals):
                total = total + part_in[order, at, s].astype(F32)
            out_ref[(i - 2) * KC + s] = total
            return 0

        lax.fori_loop(first, first + count, one, 0, unroll=4)

    make_rhs(0)
    add_block(0, 0, 1)
    far_edges = [send_edge(FAR, 0, 0, KC, 2, far)]
    make_rhs(1)
    add_block(1, 4, 2)
    for copy in near_edges:
        copy.wait()
    make_parts(0, NEAR, 5, 0, KC)
    relays0, direct0 = send_halves(0)
    add_block(0, 1, 1)
    add_block(1, 1, 1)
    for n in range(2):
        far_edges.append(send_edge(FAR, 1, n * half, half, 3 + n, far))
    add_block(0, 4, 1)
    make_parts(1, NEAR, 4, 0, KC)
    relays1, direct1 = send_halves(1)
    add_block(2, 2, 2)
    add_block(0, 2, 2)
    add_block(1, 2, 2)
    merged0 = send_merged(0, relays0)
    far_edges[0].wait()
    make_parts(2, FAR, 3, 0, KC)
    relays2, direct2 = send_halves(2)
    merged1 = send_merged(1, relays1)
    whole3 = []
    for n in range(2):
        far_edges[1 + n].wait()
        make_parts(3, FAR, 2, n * half, half)
        whole3.append(send_whole(3, n * half, half, 3 * n))
    merged2 = send_merged(2, relays2)
    finish(0, 5, 0, KC, 2, direct0 + merged0)
    finish(1, 4, 0, KC, 2, direct1 + merged1)
    finish(2, 3, 0, KC, 2, direct2 + merged2)
    for n in range(2):
        finish(3, 2, n * half, half, 3, whole3[n])
    for copy in far_halo:
        copy.wait_send()


def per_device(rows, cols, a_tiles, a_cols, p_tiles, p_cols, c_cols):
    size = BS // cols
    dma = pltpu.SemaphoreType.DMA
    hbm = pl.BlockSpec(memory_space=pl.ANY)
    out = pl.pallas_call(
        functools.partial(kernel, rows, cols),
        out_shape=pltpu.VMEM((GROUPS * KC, size, BS), F32),
        in_specs=[hbm] * 5,
        out_specs=pl.BlockSpec(memory_space=pltpu.VMEM),
        scratch_shapes=[
            pltpu.SMEM((KA, RB), jnp.int32),
            pltpu.SMEM(p_cols.shape[::-1], jnp.int32),
            pltpu.SMEM(c_cols.shape[::-1], jnp.int32),
            pltpu.VMEM((ZERO_TILE + 1, BS, BS), BF16),
            pltpu.VMEM((ZERO_TILE + 1, BS, BS), BF16),
            pltpu.VMEM((RB * KA, BS, BS), BF16),
            pltpu.VMEM((RB * (KP + 1), BS, KA * BS), BF16),
            pltpu.VMEM((GROUPS, WI * BS, GR * KA * BS), BF16),
            pltpu.VMEM((GROUPS, GR * KA * BS, WC * BS), BF16),
            pltpu.VMEM((NK + 1, NI * BS, BS), F32),
            pltpu.VMEM((2, PAIR, BS, BS), BF16),
            pltpu.VMEM((2, PAIR, BS, BS), BF16),
            pltpu.VMEM((4, KC, BS, BS), F32),
            pltpu.VMEM((4, cols, KC, size, BS), BF16),
            pltpu.VMEM((4, 2, KC // 2, size, BS), BF16),
            pltpu.VMEM((4, cols - 1, KC, size, BS), BF16),
            pltpu.VMEM((4, 2, KC // 2, size, BS), BF16),
            dma((6,)),
            dma((1,)),
            dma((1,)),
            dma((5,)),
            dma((5,)),
            dma((4,)),
            dma((4,)),
            dma((5,)),
            dma((5,)),
            dma((24,)),
            dma((24,)),
        ],
        compiler_params=pltpu.CompilerParams(
            collective_id=0, has_side_effects=True, vmem_limit_bytes=58 * 1024 * 1024
        ),
    )(
        a_cols.T, p_cols.T, c_cols.T,
        a_tiles.reshape(RB * KA, BS, BS), p_tiles.reshape(LT, BS, BS),
    )
    return out.reshape(GROUPS, KC, size, BS)


def solution(mesh):
    rows, cols = mesh.shape["row"], mesh.shape["col"]
    in_specs = (P("row", "col", None, None), P("row", "col"), P("row", None, None, None), P(), P())
    return jax.shard_map(
        functools.partial(per_device, rows, cols),
        mesh=mesh, in_specs=in_specs, out_specs=P("row", None, "col", None), check_vma=False,
    )
```

```python
import functools

import jax
import jax.numpy as jnp
from jax import lax
from jax.experimental import pallas as pl
from jax.experimental.pallas import tpu as pltpu
from jax.sharding import PartitionSpec as P

MESH = pl.DeviceIdType.MESH
BS = 128
RB = 16
KP = 3
KA = 2
KC = 8
HALO = 8
GROUPS = 4
GR = 4
WI = 5
WC = 9
NI = 8
NK = 12
HT = HALO * KP
LT = RB * KP
ZERO_TILE = HT + LT
PAIR = 2 * KC
FAR, NEAR = 0, 1
F32 = jnp.float32
BF16 = jnp.bfloat16


def select_slot(wanted, columns, values, otherwise):
    picked = jnp.int32(otherwise)
    for column, value in zip(columns, values):
        picked = jnp.where(column == wanted, value, picked)
    return picked


class Guarded:
    def __init__(self, copy, made):
        self.copy, self.made = copy, made

    def start(self):
        pl.when(self.made)(self.copy.start)

    def wait(self):
        pl.when(self.made)(self.copy.wait)

    def wait_recv(self):
        pl.when(self.made)(self.copy.wait_recv)

    def wait_send(self):
        pl.when(self.made)(self.copy.wait_send)


def tiles_at(first, count):
    return pl.ds(pl.multiple_of(first * BS, BS), count * BS)


def kernel(
    rows, cols,
    a_cols_ref, p_cols_ref, c_cols_ref, a_ref, p_ref,
    out_ref,
    ac, pc, cc, far_buf, near_buf, a_buf, left, lhs, rhs, acc,
    edge_out, edge_in, own, part_out, merged, part_in, relay_in,
    local_sem, near_send, near_recv, far_send, far_recv, hop_send, hop_recv,
    edge_send, edge_recv, part_send, part_recv,
):
    r = lax.axis_index("row")
    x = lax.axis_index("col")
    first_core = lax.rem(r, 2) == 0

    def by_core(zero, one):
        return jnp.where(first_core, zero, one)

    before = lax.rem(r + rows - 1, rows)
    after = lax.rem(r + 1, rows)
    far = by_core(before, after)
    near = by_core(after, before)
    up = lax.rem(x + 1, cols)
    across = lax.rem(x + 2, cols)
    down = lax.rem(x + 3, cols)

    has_far = by_core(r, rows - 1 - r) > 0

    def send(src, dst, sems, recv_sems, at, made=None, **device):
        copy = pltpu.make_async_remote_copy(
            src_ref=src, dst_ref=dst, send_sem=sems.at[at], recv_sem=recv_sems.at[at],
            device_id=device, device_id_type=MESH,
        )
        if made is not None:
            copy = Guarded(copy, made)
        copy.start()
        return copy

    far_rows = by_core(HT, 0)
    near_rows = by_core(0, HT)
    local = [
        pltpu.make_async_copy(src, dst, local_sem.at[i])
        for i, (src, dst) in enumerate((
            (p_ref, near_buf.at[pl.ds(near_rows, LT)]),
            (a_ref, a_buf),
            (a_cols_ref, ac),
            (p_cols_ref, pc),
            (c_cols_ref, cc),
            (p_ref, far_buf.at[pl.ds(far_rows, LT)]),
        ))
    ]
    for copy in local[:5]:
        copy.start()

    barrier = pltpu.get_barrier_semaphore()

    @pl.when(has_far)
    def _():
        pl.semaphore_signal(barrier, inc=1, device_id={"row": far}, device_id_type=MESH)

    pl.semaphore_signal(barrier, inc=1, device_id={"row": near}, device_id_type=MESH)
    for target in (up, down):
        pl.semaphore_signal(barrier, inc=1, device_id={"col": target}, device_id_type=MESH)
    pl.semaphore_wait(barrier, jnp.where(has_far, 4, 3))

    far_src = by_core(0, LT - HT)
    far_there = by_core(LT, 0)
    far_here = by_core(0, LT)
    far_halo = []
    for k, (tile, count) in enumerate((
        (4 * x, 2), (4 * x + 2, 2), (4 * across, 4), (16, 4), (20, 4)
    )):
        far_halo.append(send(
            p_ref.at[pl.ds(far_src + tile, count)], far_buf.at[pl.ds(far_there + tile, count)],
            far_send, far_recv, k, made=has_far, row=far,
        ))
    near_halo = send(
        p_ref.at[pl.ds(by_core(LT - HT, 0), HT)],
        near_buf.at[pl.ds(by_core(0, LT), HT)],
        near_send, near_recv, 0, row=near,
    )

    local[5].start()

    @pl.when(jnp.logical_not(has_far))
    def _():
        edge_in[FAR] = jnp.zeros((PAIR, BS, BS), BF16)

    far_buf[ZERO_TILE] = jnp.zeros((BS, BS), BF16)
    near_buf[ZERO_TILE] = jnp.zeros((BS, BS), BF16)

    def clear_acc(k, _):
        acc[k] = jnp.zeros((NI * BS, BS), F32)
        return 0

    lax.fori_loop(0, NK + 1, clear_acc, 0)
    local[0].wait()
    local[1].wait()

    def make_left(g, _):
        tiles = jnp.concatenate([a_buf[g * KA + a] for a in range(KA)], axis=1)
        interp = jnp.concatenate(
            [near_buf[near_rows + g * KP + p] for p in range(KP)], axis=1
        )
        product = lax.dot_general(
            interp, tiles, (((0,), (0,)), ((), ())), preferred_element_type=F32
        ).astype(BF16)
        for p in range(KP):
            left[g * (KP + 1) + p] = product[p * BS:(p + 1) * BS]
        left[g * (KP + 1) + KP] = jnp.zeros((BS, KA * BS), BF16)
        return 0

    hops = []

    def forward(k):
        far_halo[k].wait_recv()
        here = far_buf.at[pl.ds(far_here + 4 * x + 2 * k, 2)]
        for n, target in enumerate((up, down)):
            hops.append(
                send(here, here, hop_send, hop_recv, 2 * k + n, made=has_far, col=target)
            )

    lax.fori_loop(0, RB, make_left, 0, unroll=2)
    forward(0)
    for copy in local[2:]:
        copy.wait()

    def make_lhs(gi, _):
        for gg in range(GR):
            g = gi * GR + gg
            columns = [pc[p, r * RB + g] for p in range(KP)]
            for s in range(WI):
                slot = select_slot(r * GROUPS - 2 + gi + s, columns, range(KP), KP)
                lhs[gi, s * BS:(s + 1) * BS, gg * KA * BS:(gg + 1) * KA * BS] = (
                    left[g * (KP + 1) + slot]
                )
        return 0

    lax.fori_loop(0, GROUPS, make_lhs, 0)
    forward(1)
    def make_rhs(group):
        gi = by_core(group, GROUPS - 1 - group)
        if group < 2:
            buf, first_row = far_buf, r * RB - by_core(HALO, 0)
        else:
            buf, first_row = near_buf, r * RB - by_core(0, HALO)
        for gg in range(GR):
            for a in range(KA):
                j = ac[a, gi * GR + gg]
                columns = [pc[q, j] for q in range(KP)]
                first = jnp.clip(j - first_row, 0, RB + HALO - 1) * KP
                values = [first + q for q in range(KP)]
                at = (gg * KA + a) * BS
                for w in range(WC):
                    tile = select_slot(r * GROUPS - 4 + gi + w, columns, values, ZERO_TILE)
                    rhs[gi, at:at + BS, w * BS:(w + 1) * BS] = buf[tile]

    def add_block(group, row, count):
        gi = by_core(group, GROUPS - 1 - group)
        i = by_core(row, NI - row - count)
        for w in range(0, WC, 2):
            wide = min(2, WC - w)
            piece = jnp.dot(
                lhs[gi, tiles_at(i - gi, count), :], rhs[gi, :, w * BS:(w + wide) * BS],
                preferred_element_type=F32,
            )
            for u in range(wide):
                acc[gi + w + u, tiles_at(i, count), :] += piece[:, u * BS:(u + 1) * BS]

    def tile_of(row, s):
        i = jnp.clip(r * GROUPS - 2 + row, 0, rows * GROUPS - 1)
        k = cc[s, i] - (r * GROUPS - 4)
        k = jnp.where(jnp.logical_and(k >= 0, k < NK), k, NK)
        return acc[k, tiles_at(row, 1), :]

    def send_edge(side, row, first, count, order, target):
        i = by_core(row, NI - 1 - row)
        slot = lax.rem(i, 2) * KC + first

        def one(s, _):
            edge_out[side, slot + s] = tile_of(i, first + s).astype(BF16)
            return 0

        lax.fori_loop(0, count, one, 0, unroll=4)
        at = pl.ds(slot, count)
        return send(
            edge_out.at[side, at], edge_in.at[side, at], edge_send, edge_recv,
            order, made=has_far if side == FAR else None, row=target,
        )

    near_halo.wait()
    make_rhs(3)
    add_block(3, 3, 5)
    near_edges = [send_edge(NEAR, 7, 0, KC, 0, near)]
    make_rhs(2)
    add_block(2, 4, 3)
    near_edges.append(send_edge(NEAR, 6, 0, KC, 1, near))
    for copy in far_halo[2:]:
        copy.wait_recv()
    for copy in hops:
        copy.wait()
    size = BS // cols
    half = KC // 2

    def part_of(part):
        return pl.ds(pl.multiple_of(part * size, size), size)

    def make_parts(order, side, row, first, count):
        i = by_core(row, NI - 1 - row)
        slot = lax.rem(i, 2) * KC

        def one(s, _):
            total = tile_of(i, s) + edge_in[side, slot + s].astype(F32)
            own[order, s] = total
            for part in range(cols):
                part_out[order, part, s] = total[part * size:(part + 1) * size].astype(BF16)
            return 0

        lax.fori_loop(first, first + count, one, 0, unroll=4)

    def send_part(src, dst, order, at, target):
        return send(src, dst, part_send, part_recv, order * 6 + at, col=target)

    def send_halves(order):
        relays, direct = [], []
        for way, target in enumerate((up, down)):
            first, last = pl.ds(way * half, half), pl.ds((1 - way) * half, half)
            relays.append(send_part(
                part_out.at[order, across, first], relay_in.at[order, way], order, way, target
            ))
            direct.append(send_part(
                part_out.at[order, target, last], part_in.at[order, way, last],
                order, 2 + way, target,
            ))
        return relays, direct

    def send_merged(order, relays):
        copies = []
        for way, target in enumerate((up, down)):
            relays[way].wait()

            def one(n, _):
                total = own[order, way * half + n, part_of(target), :]
                merged[order, way, n] = (
                    total + relay_in[order, way, n].astype(F32)
                ).astype(BF16)
                return 0

            lax.fori_loop(0, half, one, 0, unroll=4)
            copies.append(send_part(
                merged.at[order, way], part_in.at[order, way, pl.ds(way * half, half)],
                order, 4 + way, target,
            ))
        return copies

    def send_whole(order, first, count, base):
        some = pl.ds(first, count)
        return [
            send_part(
                part_out.at[order, target, some], part_in.at[order, at, some],
                order, base + at, target,
            )
            for at, target in ((2, across), (0, up), (1, down))
        ]

    def finish(order, row, first, count, arrivals, copies):
        for copy in copies:
            copy.wait()
        i = by_core(row, NI - 1 - row)

        def one(s, _):
            total = own[order, s, part_of(x), :]
            for at in range(arrivals):
                total = total + part_in[order, at, s].astype(F32)
            out_ref[(i - 2) * KC + s] = total
            return 0

        lax.fori_loop(first, first + count, one, 0, unroll=4)

    make_rhs(0)
    add_block(0, 0, 1)
    far_edges = [send_edge(FAR, 0, 0, KC, 2, far)]
    make_rhs(1)
    add_block(1, 4, 2)
    for copy in near_edges:
        copy.wait()
    make_parts(0, NEAR, 5, 0, KC)
    relays0, direct0 = send_halves(0)
    add_block(0, 1, 1)
    add_block(1, 1, 1)
    for n in range(2):
        far_edges.append(send_edge(FAR, 1, n * half, half, 3 + n, far))
    add_block(0, 4, 1)
    make_parts(1, NEAR, 4, 0, KC)
    relays1, direct1 = send_halves(1)
    add_block(0, 2, 2)
    add_block(1, 2, 2)
    add_block(2, 2, 2)
    merged0 = send_merged(0, relays0)
    far_edges[0].wait()
    make_parts(2, FAR, 3, 0, KC)
    relays2, direct2 = send_halves(2)
    merged1 = send_merged(1, relays1)
    whole3 = []
    for n in range(2):
        far_edges[1 + n].wait()
        make_parts(3, FAR, 2, n * half, half)
        whole3.append(send_whole(3, n * half, half, 3 * n))
    merged2 = send_merged(2, relays2)
    finish(0, 5, 0, KC, 2, direct0 + merged0)
    finish(1, 4, 0, KC, 2, direct1 + merged1)
    finish(2, 3, 0, KC, 2, direct2 + merged2)
    for n in range(2):
        finish(3, 2, n * half, half, 3, whole3[n])
    for copy in far_halo:
        copy.wait_send()


def per_device(rows, cols, a_tiles, a_cols, p_tiles, p_cols, c_cols):
    size = BS // cols
    dma = pltpu.SemaphoreType.DMA
    hbm = pl.BlockSpec(memory_space=pl.ANY)
    out = pl.pallas_call(
        functools.partial(kernel, rows, cols),
        out_shape=pltpu.VMEM((GROUPS * KC, size, BS), F32),
        in_specs=[hbm] * 5,
        out_specs=pl.BlockSpec(memory_space=pltpu.VMEM),
        scratch_shapes=[
            pltpu.SMEM((KA, RB), jnp.int32),
            pltpu.SMEM(p_cols.shape[::-1], jnp.int32),
            pltpu.SMEM(c_cols.shape[::-1], jnp.int32),
            pltpu.VMEM((ZERO_TILE + 1, BS, BS), BF16),
            pltpu.VMEM((ZERO_TILE + 1, BS, BS), BF16),
            pltpu.VMEM((RB * KA, BS, BS), BF16),
            pltpu.VMEM((RB * (KP + 1), BS, KA * BS), BF16),
            pltpu.VMEM((GROUPS, WI * BS, GR * KA * BS), BF16),
            pltpu.VMEM((GROUPS, GR * KA * BS, WC * BS), BF16),
            pltpu.VMEM((NK + 1, NI * BS, BS), F32),
            pltpu.VMEM((2, PAIR, BS, BS), BF16),
            pltpu.VMEM((2, PAIR, BS, BS), BF16),
            pltpu.VMEM((4, KC, BS, BS), F32),
            pltpu.VMEM((4, cols, KC, size, BS), BF16),
            pltpu.VMEM((4, 2, KC // 2, size, BS), BF16),
            pltpu.VMEM((4, cols - 1, KC, size, BS), BF16),
            pltpu.VMEM((4, 2, KC // 2, size, BS), BF16),
            dma((6,)),
            dma((1,)),
            dma((1,)),
            dma((5,)),
            dma((5,)),
            dma((4,)),
            dma((4,)),
            dma((5,)),
            dma((5,)),
            dma((24,)),
            dma((24,)),
        ],
        compiler_params=pltpu.CompilerParams(
            collective_id=0, has_side_effects=True, vmem_limit_bytes=58 * 1024 * 1024
        ),
    )(
        a_cols.T, p_cols.T, c_cols.T,
        a_tiles.reshape(RB * KA, BS, BS), p_tiles.reshape(LT, BS, BS),
    )
    return out.reshape(GROUPS, KC, size, BS)


def solution(mesh):
    rows, cols = mesh.shape["row"], mesh.shape["col"]
    in_specs = (P("row", "col", None, None), P("row", "col"), P("row", None, None, None), P(), P())
    return jax.shard_map(
        functools.partial(per_device, rows, cols),
        mesh=mesh, in_specs=in_specs, out_specs=P("row", None, "col", None), check_vma=False,
    )
```
